768 devices in a mesh: blk: 16 (over x, y_hi, core), dp: 48 (over z, y_lo).
Axes of the slice: x: 4, y: 8 (y_hi: 2, y_lo: 4; y = y_hi * 4 + y_lo), z: 12, core: 2. Of those that a mesh axis runs over, the one named last changes fastest.
Arguments:
- acts: bfloat16 [98304, 4096], P(('blk', 'dp')), may hold values from -6 to 6
- cotangent: bfloat16 [98304, 512], P(('blk', 'dp')), may hold values from -6 to 6
- kv_weight: bfloat16 [4096, 512], P('blk'), may hold values from -0.09375 to 0.09375
- batch_counts: int32 [768], P(('blk', 'dp')), may hold values from 1 to 4, as said below
Outputs:
- projected: bfloat16 [98304, 512], P(('blk', 'dp'))
- act_grad: bfloat16 [98304, 4096], P(('blk', 'dp'))
- weight_grad: float32 [4096, 512], P('blk')
The draws below stay inside these ranges and needn't reach their ends.
Inputs may be any that keep to these rules, and one draw needn't show every extreme that they name: `batch_counts`: some worker has all 4 micro-batches live and some worker only one.
All inputs are finite; a program needn't handle non-finite values.
Results may differ from the reference program's by a relative error of at most 0.001.
Values may be sent and summed in bfloat16 or wider, within the bound.
No kernel may reach another device: no remote copies, remote signals or barrier semaphores. Data moves between devices by JAX's collectives and lax.ppermute only.
A program may use at most 32 MiB of HBM per device.

```python
import jax
import jax.numpy as jnp

DIN = 4096
MICRO = 32
TOK_DEV = 128
HD = 512
BATCHES = 4
WORKERS = 768
TOKENS = 98304


def draw_batch_counts(key, part):
    key = jax.random.fold_in(key, 7)
    counts = jax.random.randint(key, (WORKERS,), 1, BATCHES + 1).astype(jnp.int32)
    counts = counts.at[0].set(BATCHES)
    counts = counts.at[1].set(1)
    return counts


def shard_levels(stream_key, extent, shards, smallest, high):
    level = 1.0
    for dim, shards_of in shards:
        draws = jax.random.uniform(jax.random.fold_in(jax.random.fold_in(stream_key, 6), dim), (shards_of,), jnp.float32, smallest / len(shards), high / len(shards))
        level = level * jnp.repeat(jnp.exp(draws), extent[dim] // shards_of).reshape((-1,) + (1,) * (len(extent) - 1 - dim))
    return level


def bell_draw(stream_key, shape, scale, bound, cuts=(), kind=jnp.bfloat16):
    loudness = shard_levels(stream_key, shape, cuts, -0.22, 0.18) if cuts else 1.0
    values = jax.random.normal(stream_key, shape, jnp.float32) * scale * loudness
    return jnp.minimum(jnp.maximum(values, -bound), bound).astype(kind)


def setup_inputs(seed: int = 0) -> dict:
    streams_of = jax.random.split(jax.random.key(seed), 5)
    acts = bell_draw(streams_of[0], (TOKENS, DIN), 1.0, 6.0, ((0, 768),))
    cotangent = bell_draw(streams_of[1], (TOKENS, HD), 1.0, 6.0, ((0, 768),))
    kv_weight = bell_draw(streams_of[2], (DIN, HD), DIN ** -0.5, 0.09375, ((0, 16),))
    batch_counts = draw_batch_counts(jax.random.fold_in(streams_of[4], 71), 0)
    return dict(acts=acts, cotangent=cotangent, kv_weight=kv_weight, batch_counts=batch_counts)


def reference(acts, cotangent, kv_weight, batch_counts):
    rows = jnp.arange(TOK_DEV, dtype=jnp.int32)
    live = (rows[None, :] < batch_counts[:, None] * MICRO).astype(jnp.float32)
    live = live.reshape(TOKENS, 1)
    projected = (jnp.dot(acts, kv_weight, preferred_element_type=jnp.float32) * live).astype(jnp.bfloat16)
    masked = (cotangent.astype(jnp.float32) * live).astype(jnp.bfloat16)
    act_grad = jnp.dot(masked, kv_weight.T, preferred_element_type=jnp.float32).astype(jnp.bfloat16)
    total = jnp.dot(acts.T, masked, preferred_element_type=jnp.float32)
    weight_grad = total * (float(TOKENS) ** -0.5)
    return projected, act_grad, weight_grad
```

```python
import functools

import jax
import jax.numpy as jnp
from jax import lax
from jax.experimental import pallas as pl
from jax.experimental.pallas import tpu as pltpu
from jax.sharding import Mesh, PartitionSpec as P

MICRO = 32
X, YH, CORE, ZH, ZL, YL = 4, 2, 2, 3, 4, 4
SIZES = (X, YH, CORE, ZH, ZL, YL)
NAMES = ("x", "yh", "core", "zh", "zl", "yl")
TOK, DIN, HD = 128, 4096, 512
SHARD = DIN // (X * YH * CORE)
PEERS = X * CORE
PIECES = YH * ZL * YL
ROWS = SHARD // (ZL * YL)
SCALE = float(TOK * X * YH * CORE * ZH * ZL * YL) ** -0.5

VMEM = pl.BlockSpec(memory_space=pltpu.VMEM)
SMEM = pl.BlockSpec(memory_space=pltpu.SMEM)
PARAMS = pltpu.CompilerParams(vmem_limit_bytes=40 * 1024 * 1024)


def pack_kernel(counts, acts, cot, out, masked):
    rows = lax.broadcasted_iota(jnp.int32, (TOK, HD), 0)
    kept = jnp.where(rows < counts[0] * MICRO, cot[...].astype(jnp.float32), 0.0)
    kept = kept.astype(jnp.bfloat16)
    masked[...] = kept
    for x in range(X):
        for c in range(CORE):
            peer = x * CORE + c
            for yh in range(YH):
                b = (x * YH + yh) * CORE + c
                out[peer, 0:TOK, yh * SHARD:(yh + 1) * SHARD] = acts[:, b * SHARD:(b + 1) * SHARD]
            out[peer, TOK:2 * TOK, :] = kept


def grad_kernel(place, got, own, near, far, out, pair):
    cols = 128
    right = got[:, TOK:2 * TOK, :].reshape(PEERS * TOK, HD)
    for i in range(YH * SHARD // cols):
        left = got[:, 0:TOK, i * cols:(i + 1) * cols].reshape(PEERS * TOK, cols)
        part = lax.dot_general(left, right, (((0,), (0,)), ((), ())), preferred_element_type=jnp.float32)
        out[i * (cols // ROWS):(i + 1) * (cols // ROWS)] = part.reshape(cols // ROWS, ROWS, HD)
    yh, yl = place[0], place[1]
    pair[yh] = own[...]

    @pl.when((yl == 0) | (yl == YL - 1))
    def _():
        pair[1 - yh] = near[...]

    @pl.when((yl != 0) & (yl != YL - 1))
    def _():
        pair[1 - yh] = far[...]


def project_kernel(place, counts, acts, masked, w0, w1, w2, w3, other, projected, act_grad):
    x, c = place[0], place[1]
    total = jnp.zeros((TOK, HD), jnp.float32)
    mk = masked[...]
    mine = (w0, w1, w2, w3)
    for k in range(X):
        xs = lax.rem(x - k + X, X)
        for side in range(CORE):
            cs = c if side == 0 else 1 - c
            for yh in range(YH):
                w = mine[k][yh] if side == 0 else other[k, yh]
                start = pl.multiple_of(((xs * YH + yh) * CORE + cs) * SHARD, SHARD)
                total += jnp.dot(acts[:, pl.ds(start, SHARD)], w, preferred_element_type=jnp.float32)
                back = lax.dot_general(mk, w, (((1,), (1,)), ((), ())), preferred_element_type=jnp.float32)
                act_grad[:, pl.ds(start, SHARD)] = back.astype(jnp.bfloat16)
    rows = lax.broadcasted_iota(jnp.int32, (TOK, HD), 0)
    projected[...] = jnp.where(rows < counts[0] * MICRO, total, 0.0).astype(jnp.bfloat16)


def sds(shape, dtype):
    return jax.ShapeDtypeStruct(shape, dtype)


def y_permute(value, pairs):
    return lax.ppermute(value, ("yh", "yl"), pairs)


def spread(piece, axes, count):
    return lax.all_to_all(jnp.broadcast_to(piece[None], (count,) + piece.shape), axes, 0, 0, tiled=True)


def per_device(acts, cotangent, kv_weight, batch_counts):
    x, c = lax.axis_index("x"), lax.axis_index("core")
    yh, yl = lax.axis_index("yh"), lax.axis_index("yl")
    bf16, f32 = jnp.bfloat16, jnp.float32

    near = y_permute(kv_weight, [(4, 3), (7, 0), (3, 4), (0, 7)])
    far = y_permute(kv_weight, [(4, 2), (7, 1), (3, 5), (0, 6)])

    packed, masked = pl.pallas_call(
        pack_kernel,
        out_shape=(sds((PEERS, 2 * TOK, HD), bf16), sds((TOK, HD), bf16)),
        in_specs=[SMEM, VMEM, VMEM],
        out_specs=(VMEM, VMEM),
        compiler_params=PARAMS,
        name="pack",
    )(batch_counts, acts, cotangent)
    got = lax.all_to_all(packed, ("x", "core"), 0, 0, tiled=True)

    partial, pair = pl.pallas_call(
        grad_kernel,
        out_shape=(sds((PIECES, ROWS, HD), f32), sds((YH, SHARD, HD), bf16)),
        in_specs=[SMEM, VMEM, VMEM, VMEM, VMEM],
        out_specs=(VMEM, VMEM),
        compiler_params=PARAMS,
        name="grad",
    )(jnp.stack([yh, yl]), got, kv_weight, near, far)

    parts = lax.all_to_all(partial, ("yh", "zl", "yl"), 0, 0, tiled=True)

    turned = [lax.ppermute(pair, "x", [(i, (i + k) % X) for i in range(X)]) for k in range(1, X)]
    line = jnp.stack([pair] + turned)
    other = lax.ppermute(line, "core", [(0, 1), (1, 0)])

    piece = jnp.sum(parts, axis=0) * SCALE
    piece = jnp.sum(spread(piece, "zh", ZH), axis=0)
    weight_grad = spread(piece, ("zl", "yl"), ZL * YL).reshape(SHARD, HD)

    projected, act_grad = pl.pallas_call(
        project_kernel,
        out_shape=(sds((TOK, HD), bf16), sds((TOK, DIN), bf16)),
        in_specs=[SMEM, SMEM] + [VMEM] * 7,
        out_specs=(VMEM, VMEM),
        compiler_params=PARAMS,
        name="project",
    )(jnp.stack([x, c]), batch_counts, acts, masked, pair, *turned, other)
    return projected, act_grad, weight_grad


def solution(mesh):
    inner = Mesh(mesh.devices.reshape(SIZES), NAMES)
    return jax.shard_map(
        per_device,
        mesh=inner,
        in_specs=(P(NAMES, None), P(NAMES, None), P(("x", "yh", "core"), None), P(NAMES)),
        out_specs=(P(NAMES, None), P(NAMES, None), P(("x", "yh", "core"), None)),
        check_vma=False,
    )
```

```python
import jax
import jax.numpy as jnp
from jax import lax
from jax.experimental import pallas as pl
from jax.experimental.pallas import tpu as pltpu
from jax.sharding import Mesh, PartitionSpec as P

MICRO = 32
X, YH, CORE, ZH, ZL, YL = 4, 2, 2, 3, 4, 4
SIZES = (X, YH, CORE, ZH, ZL, YL)
NAMES = ("x", "yh", "core", "zh", "zl", "yl")
TOK, DIN, HD = 128, 4096, 512
SHARD = DIN // (X * YH * CORE)
PEERS = X * CORE
PIECES = YH * ZL * YL
ROWS = SHARD // (ZL * YL)
LANES = 128
FLAT = ROWS * HD // LANES
TALL = FLAT + 8
SCALE = float(TOK * X * YH * CORE * ZH * ZL * YL) ** -0.5
TOP = 13.0

VMEM = pl.BlockSpec(memory_space=pltpu.VMEM)
SMEM = pl.BlockSpec(memory_space=pltpu.SMEM)
ANY = pl.BlockSpec(memory_space=pl.ANY)
TINY, SMALL, LARGE = 8 * 1024 * 1024, 16 * 1024 * 1024, 60 * 1024 * 1024
bf16, f16, f32 = jnp.bfloat16, jnp.float16, jnp.float32


def pack_kernel(counts, acts, cot, packed, masked, raw, kept, full, built, sems):
    wide = DIN // X
    first = pltpu.make_async_copy(cot, raw, sems.at[0])
    first.start()
    loads = [
        pltpu.make_async_copy(
            acts.at[:, x * wide:(x + 1) * wide], full.at[:, x * wide:(x + 1) * wide], sems.at[1 + x])
        for x in range(X)
    ]
    for load in loads:
        load.start()
    first.wait()
    rows = lax.broadcasted_iota(jnp.int32, (TOK, HD), 0)
    kept[...] = jnp.where(rows < counts[0] * MICRO, raw[...].astype(f32), 0.0).astype(bf16)
    stores = [pltpu.make_async_copy(kept, masked, sems.at[1 + X])]
    stores[0].start()
    for x in range(X):
        loads[x].wait()
        for side in range(CORE):
            peer = x * CORE + side
            for yh in range(YH):
                b = (x * YH + yh) * CORE + side
                built[peer, 0:TOK, yh * SHARD:(yh + 1) * SHARD] = full[:, b * SHARD:(b + 1) * SHARD]
            built[peer, TOK:2 * TOK, :] = kept[...]
        pieces = slice(x * CORE, (x + 1) * CORE)
        stores.append(pltpu.make_async_copy(built.at[pieces], packed.at[pieces], sems.at[2 + X + x]))
        stores[-1].start()
    for store in stores:
        store.wait()


def exponent(values):
    top = jnp.max(jnp.max(jnp.abs(values), axis=1, keepdims=True), axis=0, keepdims=True)
    return TOP - jnp.floor(jnp.log2(jnp.maximum(top, 2.0 ** -100)))


def encode(out, i, rows, power):
    for j in range(HD // LANES):
        out[i, j * ROWS:(j + 1) * ROWS, :] = rows[:, j * LANES:(j + 1) * LANES]
    out[i, FLAT:TALL, :] = jnp.broadcast_to(power, (TALL - FLAT, LANES))


def decode(ref, i):
    return ref[i, 0:FLAT, :] * jnp.exp2(-ref[i, FLAT:FLAT + 1, :])


def grad_kernel(got, pair, out, same, acc):
    cols = 128
    right = got[:, TOK:2 * TOK, :].reshape(PEERS * TOK, HD)
    for i in range(YH * SHARD // cols):
        left = got[:, 0:TOK, i * cols:(i + 1) * cols].reshape(PEERS * TOK, cols)
        acc[i * cols:(i + 1) * cols, :] = lax.dot_general(
            left, right, (((0,), (0,)), ((), ())), preferred_element_type=f32)
    power = exponent(acc[...])
    factor = jnp.exp2(power)
    for i in range(PIECES):
        encode(out, i, acc[i * ROWS:(i + 1) * ROWS, :] * factor, power)


def sum_kernel(parts, out):
    total = decode(parts, 0)
    for i in range(1, PIECES):
        total += decode(parts, i)
    for i in range(ZH):
        out[i] = total


def final_kernel(parts, out):
    total = parts[0]
    for i in range(1, ZH):
        total += parts[i]
    total = total * SCALE
    power = exponent(total)
    total = total * jnp.exp2(power)
    for i in range(ZL * YL):
        out[i, 0:FLAT, :] = total
        out[i, FLAT:TALL, :] = jnp.broadcast_to(power, (TALL - FLAT, LANES))


def unpack_kernel(got, out):
    for i in range(ZL * YL):
        value = decode(got, i)
        for j in range(HD // LANES):
            out[i * ROWS:(i + 1) * ROWS, j * LANES:(j + 1) * LANES] = value[j * ROWS:(j + 1) * ROWS, :]


def project_kernel(place, counts, acts, masked, after, w0, w1, w2, w3, projected, act_grad):
    x = place[0]
    kept = masked[...]
    total = jnp.zeros((TOK, HD), f32)
    for k, shards in enumerate((w0, w1, w2, w3)):
        group = lax.rem(x - k + X, X) * YH * CORE
        for core in range(CORE):
            for yh in range(YH):
                w = shards[core, yh]
                start = pl.multiple_of((group + yh * CORE + core) * SHARD, SHARD)
                total += jnp.dot(acts[:, pl.ds(start, SHARD)], w, preferred_element_type=f32)
                back = lax.dot_general(kept, w, (((1,), (1,)), ((), ())), preferred_element_type=f32)
                act_grad[:, pl.ds(start, SHARD)] = back.astype(bf16)
    rows = lax.broadcasted_iota(jnp.int32, (TOK, HD), 0)
    projected[...] = jnp.where(rows < counts[0] * MICRO, total, 0.0).astype(bf16)


def sds(shape, dtype):
    return jax.ShapeDtypeStruct(shape, dtype)


def call(body, outs, ins, out_specs, scratch=(), name=None, limit=SMALL, **more):
    return pl.pallas_call(
        body, out_shape=outs, in_specs=ins, out_specs=out_specs, scratch_shapes=list(scratch),
        compiler_params=pltpu.CompilerParams(vmem_limit_bytes=limit), name=name, **more)


def exchange(value, axes):
    return lax.all_to_all(value, axes, 0, 0, tiled=True)


def per_device(acts, cotangent, kv_weight, batch_counts):
    x, core = lax.axis_index("x"), lax.axis_index("core")
    yh, yl = lax.axis_index("yh"), lax.axis_index("yl")
    dma = pltpu.SemaphoreType.DMA

    packed, masked = call(
        pack_kernel, (sds((PEERS, 2 * TOK, HD), bf16), sds((TOK, HD), bf16)),
        [SMEM, ANY, ANY], (ANY, ANY),
        (pltpu.VMEM((TOK, HD), bf16), pltpu.VMEM((TOK, HD), bf16), pltpu.VMEM((TOK, DIN), bf16),
         pltpu.VMEM((PEERS, 2 * TOK, HD), bf16), dma((2 + 2 * X,))),
        "pack", LARGE,
    )(batch_counts, acts, cotangent)
    got = exchange(packed, ("x", "core"))

    near = lax.ppermute(kv_weight, ("yh", "yl"), [(4, 3), (7, 0), (3, 4), (0, 7)])
    far = lax.ppermute(kv_weight, ("yh", "yl"), [(4, 2), (7, 1), (3, 5), (0, 6)])
    twin = jnp.where((yl == 0) | (yl == YL - 1), near, far)
    pair = jnp.where(yh == 0, jnp.stack([kv_weight, twin]), jnp.stack([twin, kv_weight]))
    side = lax.ppermute(pair, "core", [(0, 1), (1, 0)])
    quad = jnp.where(core == 0, jnp.stack([pair, side]), jnp.stack([side, pair]))

    partial, quad = call(
        grad_kernel, (sds((PIECES, TALL, LANES), f32), sds((CORE, YH, SHARD, HD), bf16)),
        [VMEM, ANY], (VMEM, ANY), (pltpu.VMEM((YH * SHARD, HD), f32),), "grad",
        input_output_aliases={1: 1},
    )(got, quad)
    parts = exchange(partial.astype(f16), ("yh", "zl", "yl"))
    turned = [lax.ppermute(quad, "x", [(i, (i + k) % X) for i in range(X)]) for k in range(1, X)]
    piece = call(sum_kernel, sds((ZH, FLAT, LANES), f32), [VMEM], VMEM, name="sum", limit=TINY)(parts.astype(f32))
    pieces = exchange(piece, "zh")
    ready = call(
        final_kernel, sds((ZL * YL, TALL, LANES), f32), [VMEM], VMEM, name="final", limit=TINY)(pieces)
    whole = exchange(ready.astype(f16), ("zl", "yl"))

    projected, act_grad = call(
        project_kernel, (sds((TOK, HD), bf16), sds((TOK, DIN), bf16)),
        [SMEM, SMEM, VMEM, VMEM, ANY] + [VMEM] * 4, (VMEM, VMEM), (), "project", SMALL,
        cost_estimate=pl.CostEstimate(
            flops=4 * TOK * DIN * HD, bytes_accessed=2 * (2 * TOK * DIN + DIN * HD), transcendentals=0),
    )(x.reshape(1), batch_counts, acts, masked, ready, quad, *turned)

    weight_grad = call(
        unpack_kernel, sds((SHARD, HD), f32), [VMEM], VMEM, name="unpack", limit=TINY)(whole.astype(f32))
    return projected, act_grad, weight_grad


def solution(mesh):
    inner = Mesh(mesh.devices.reshape(SIZES), NAMES)
    return jax.shard_map(
        per_device,
        mesh=inner,
        in_specs=(P(NAMES, None), P(NAMES, None), P(("x", "yh", "core"), None), P(NAMES)),
        out_specs=(P(NAMES, None), P(NAMES, None), P(("x", "yh", "core"), None)),
        check_vma=False,
    )
```

```python
import jax
import jax.numpy as jnp
from jax import lax
from jax.experimental import pallas as pl
from jax.experimental.pallas import tpu as pltpu
from jax.sharding import Mesh, PartitionSpec as P

MICRO = 32
X, YH, CORE, ZH, ZL, YL = 4, 2, 2, 3, 4, 4
SIZES = (X, YH, CORE, ZH, ZL, YL)
NAMES = ("x", "yh", "core", "zh", "zl", "yl")
TOK, DIN, HD = 128, 4096, 512
SHARD = DIN // (X * YH * CORE)
PEERS = X * CORE
HALF = DIN // CORE
PIECES = YH * ZL * YL
ROWS = SHARD // (ZL * YL)
LANES = 128
FLAT = ROWS * HD // LANES
TALL = FLAT + 8
SCALE = float(TOK * X * YH * CORE * ZH * ZL * YL) ** -0.5
TOP = 13.0
SWAP = [(0, 1), (1, 0)]

VMEM = pl.BlockSpec(memory_space=pltpu.VMEM)
SMEM = pl.BlockSpec(memory_space=pltpu.SMEM)
ANY = pl.BlockSpec(memory_space=pl.ANY)
TINY, SMALL, LARGE = 8 * 1024 * 1024, 16 * 1024 * 1024, 60 * 1024 * 1024
bf16, f16, f32 = jnp.bfloat16, jnp.float16, jnp.float32


def pack_kernel(place, counts, acts, cot, packed, masked, lend, raw, kept, full, built, loan, sems):
    wide = DIN // X
    away = 1 - place[0]
    first = pltpu.make_async_copy(cot, raw, sems.at[0])
    first.start()
    loads = [
        pltpu.make_async_copy(
            acts.at[:, x * wide:(x + 1) * wide], full.at[:, x * wide:(x + 1) * wide], sems.at[1 + x])
        for x in range(X)
    ]
    for load in loads:
        load.start()
    first.wait()
    rows = lax.broadcasted_iota(jnp.int32, (TOK, HD), 0)
    kept[...] = jnp.where(rows < counts[0] * MICRO, raw[...].astype(f32), 0.0).astype(bf16)
    stores = [pltpu.make_async_copy(kept, masked, sems.at[1 + X])]
    stores[0].start()
    for x in range(X):
        loads[x].wait()
        for side in range(CORE):
            peer = x * CORE + side
            for yh in range(YH):
                b = (x * YH + yh) * CORE + side
                built[peer, 0:TOK, yh * SHARD:(yh + 1) * SHARD] = full[:, b * SHARD:(b + 1) * SHARD]
            built[peer, TOK:2 * TOK, :] = kept[...]
        for yh in range(YH):
            start = pl.multiple_of(((x * YH + yh) * CORE + away) * SHARD, SHARD)
            loan[:, (x * YH + yh) * SHARD:(x * YH + yh + 1) * SHARD] = full[:, pl.ds(start, SHARD)]
        pieces = slice(x * CORE, (x + 1) * CORE)
        stores.append(pltpu.make_async_copy(built.at[pieces], packed.at[pieces], sems.at[2 + X + x]))
        stores[-1].start()
    loan[:, HALF:HALF + HD] = kept[...]
    stores.append(pltpu.make_async_copy(loan, lend, sems.at[2 + 2 * X]))
    stores[-1].start()
    for store in stores:
        store.wait()


def exponent(values):
    top = jnp.max(jnp.max(jnp.abs(values), axis=1, keepdims=True), axis=0, keepdims=True)
    return TOP - jnp.floor(jnp.log2(jnp.maximum(top, 2.0 ** -100)))


def encode(out, i, rows, power):
    for j in range(HD // LANES):
        out[i, j * ROWS:(j + 1) * ROWS, :] = rows[:, j * LANES:(j + 1) * LANES]
    out[i, FLAT:TALL, :] = jnp.broadcast_to(power, (TALL - FLAT, LANES))


def decode(ref, i):
    return ref[i, 0:FLAT, :] * jnp.exp2(-ref[i, FLAT:FLAT + 1, :])


def grad_kernel(got, pair, loan, out, same, same_loan, acc):
    cols = 128
    right = got[:, TOK:2 * TOK, :].reshape(PEERS * TOK, HD)
    for i in range(YH * SHARD // cols):
        left = got[:, 0:TOK, i * cols:(i + 1) * cols].reshape(PEERS * TOK, cols)
        acc[i * cols:(i + 1) * cols, :] = lax.dot_general(
            left, right, (((0,), (0,)), ((), ())), preferred_element_type=f32)
    power = exponent(acc[...])
    factor = jnp.exp2(power)
    for i in range(PIECES):
        encode(out, i, acc[i * ROWS:(i + 1) * ROWS, :] * factor, power)


def sum_kernel(parts, out):
    total = decode(parts, 0)
    for i in range(1, PIECES):
        total += decode(parts, i)
    for i in range(ZH):
        out[i] = total


def final_kernel(parts, out):
    total = parts[0]
    for i in range(1, ZH):
        total += parts[i]
    total = total * SCALE
    power = exponent(total)
    total = total * jnp.exp2(power)
    for i in range(ZL * YL):
        out[i, 0:FLAT, :] = total
        out[i, FLAT:TALL, :] = jnp.broadcast_to(power, (TALL - FLAT, LANES))


def unpack_kernel(got, out):
    for i in range(ZL * YL):
        value = decode(got, i)
        for j in range(HD // LANES):
            out[i * ROWS:(i + 1) * ROWS, j * LANES:(j + 1) * LANES] = value[j * ROWS:(j + 1) * ROWS, :]


def project_kernel(place, acts, masked, loan, after, w0, w1, w2, w3, part, grad, grad_away):
    x, core = place[0], place[1]
    kept = jnp.concatenate([masked[...], loan[:, HALF:HALF + HD]], axis=0)
    total = jnp.zeros((2 * TOK, HD), f32)
    for k, shards in enumerate((w0, w1, w2, w3)):
        group = lax.rem(x - k + X, X) * YH
        for yh in range(YH):
            w = shards[yh]
            near = pl.multiple_of(((group + yh) * CORE + core) * SHARD, SHARD)
            far = pl.multiple_of((group + yh) * SHARD, SHARD)
            rows = jnp.concatenate([acts[:, pl.ds(near, SHARD)], loan[:, pl.ds(far, SHARD)]], axis=0)
            total += jnp.dot(rows, w, preferred_element_type=f32)
            back = lax.dot_general(kept, w, (((1,), (1,)), ((), ())), preferred_element_type=f32).astype(bf16)
            cols = slice((k * YH + yh) * SHARD, (k * YH + yh + 1) * SHARD)
            grad[:, cols] = back[0:TOK]
            grad_away[:, cols] = back[TOK:2 * TOK]
    part[...] = total[0:TOK]
    top = total[TOK:2 * TOK].astype(bf16)
    grad_away[:, HALF:HALF + HD] = top
    grad_away[:, HALF + HD:HALF + 2 * HD] = (total[TOK:2 * TOK] - top.astype(f32)).astype(bf16)


def join_kernel(place, counts, part, grad, grad_away, projected, act_grad):
    x, core = place[0], place[1]
    rows = lax.broadcasted_iota(jnp.int32, (TOK, HD), 0)
    top = grad_away[:, HALF:HALF + HD].astype(f32)
    rest = grad_away[:, HALF + HD:HALF + 2 * HD].astype(f32)
    total = part[...] + (top + rest)
    projected[...] = jnp.where(rows < counts[0] * MICRO, total, 0.0).astype(bf16)
    for k in range(X):
        group = lax.rem(x - k + X, X) * YH
        for yh in range(YH):
            cols = slice((k * YH + yh) * SHARD, (k * YH + yh + 1) * SHARD)
            near = pl.multiple_of(((group + yh) * CORE + core) * SHARD, SHARD)
            far = pl.multiple_of(((group + yh) * CORE + 1 - core) * SHARD, SHARD)
            act_grad[:, pl.ds(near, SHARD)] = grad[:, cols]
            act_grad[:, pl.ds(far, SHARD)] = grad_away[:, cols]


def sds(shape, dtype):
    return jax.ShapeDtypeStruct(shape, dtype)


def call(body, outs, ins, out_specs, scratch=(), name=None, limit=SMALL, **more):
    return pl.pallas_call(
        body, out_shape=outs, in_specs=ins, out_specs=out_specs, scratch_shapes=list(scratch),
        compiler_params=pltpu.CompilerParams(vmem_limit_bytes=limit), name=name, **more)


def exchange(value, axes):
    return lax.all_to_all(value, axes, 0, 0, tiled=True)


def per_device(acts, cotangent, kv_weight, batch_counts):
    x, core = lax.axis_index("x"), lax.axis_index("core")
    yh, yl = lax.axis_index("yh"), lax.axis_index("yl")
    dma = pltpu.SemaphoreType.DMA

    packed, masked, lend = call(
        pack_kernel,
        (sds((PEERS, 2 * TOK, HD), bf16), sds((TOK, HD), bf16), sds((TOK, HALF + HD), bf16)),
        [SMEM, SMEM, ANY, ANY], (ANY, ANY, ANY),
        (pltpu.VMEM((TOK, HD), bf16), pltpu.VMEM((TOK, HD), bf16), pltpu.VMEM((TOK, DIN), bf16),
         pltpu.VMEM((PEERS, 2 * TOK, HD), bf16), pltpu.VMEM((TOK, HALF + HD), bf16), dma((3 + 2 * X,))),
        "pack", LARGE,
    )(core.reshape(1), batch_counts, acts, cotangent)
    got = exchange(packed, ("x", "core"))

    near = lax.ppermute(kv_weight, ("yh", "yl"), [(4, 3), (7, 0), (3, 4), (0, 7)])
    far = lax.ppermute(kv_weight, ("yh", "yl"), [(4, 2), (7, 1), (3, 5), (0, 6)])
    twin = jnp.where((yl == 0) | (yl == YL - 1), near, far)
    pair = jnp.where(yh == 0, jnp.stack([kv_weight, twin]), jnp.stack([twin, kv_weight]))
    loan = lax.ppermute(lend, "core", SWAP)

    partial, pair, loan = call(
        grad_kernel,
        (sds((PIECES, TALL, LANES), f32), sds((YH, SHARD, HD), bf16), sds((TOK, HALF + HD), bf16)),
        [VMEM, ANY, ANY], (VMEM, ANY, ANY), (pltpu.VMEM((YH * SHARD, HD), f32),), "grad",
        input_output_aliases={1: 1, 2: 2},
    )(got, pair, loan)

    parts = exchange(partial.astype(f16), ("yh", "zl", "yl"))
    turned = [lax.ppermute(pair, "x", [(i, (i + k) % X) for i in range(X)]) for k in range(1, X)]
    piece = call(sum_kernel, sds((ZH, FLAT, LANES), f32), [VMEM], VMEM, name="sum", limit=TINY)(parts.astype(f32))
    pieces = exchange(piece, "zh")
    ready = call(
        final_kernel, sds((ZL * YL, TALL, LANES), f32), [VMEM], VMEM, name="final", limit=TINY)(pieces)
    whole = exchange(ready.astype(f16), ("zl", "yl"))

    place = jnp.stack([x, core])
    part, grad, grad_away = call(
        project_kernel,
        (sds((TOK, HD), f32), sds((TOK, HALF), bf16), sds((TOK, HALF + 2 * HD), bf16)),
        [SMEM, VMEM, VMEM, VMEM, ANY] + [VMEM] * 4, (VMEM,) * 3, (), "project", SMALL,
        cost_estimate=pl.CostEstimate(
            flops=4 * TOK * DIN * HD, bytes_accessed=2 * (2 * TOK * DIN + DIN * HD), transcendentals=0),
    )(place, acts, masked, loan, piece, pair, *turned)
    grad_away = lax.ppermute(grad_away, "core", SWAP)
    projected, act_grad = call(
        join_kernel, (sds((TOK, HD), bf16), sds((TOK, DIN), bf16)),
        [SMEM, SMEM] + [VMEM] * 3, (VMEM, VMEM), (), "join", SMALL,
    )(place, batch_counts, part, grad, grad_away)

    weight_grad = call(
        unpack_kernel, sds((SHARD, HD), f32), [VMEM], VMEM, name="unpack", limit=TINY)(whole.astype(f32))
    return projected, act_grad, weight_grad


def solution(mesh):
    inner = Mesh(mesh.devices.reshape(SIZES), NAMES)
    return jax.shard_map(
        per_device,
        mesh=inner,
        in_specs=(P(NAMES, None), P(NAMES, None), P(("x", "yh", "core"), None), P(NAMES)),
        out_specs=(P(NAMES, None), P(NAMES, None), P(("x", "yh", "core"), None)),
        check_vma=False,
    )
```

```python
import jax
import jax.numpy as jnp
from jax import lax
from jax.experimental import pallas as pl
from jax.experimental.pallas import tpu as pltpu
from jax.sharding import Mesh, PartitionSpec as P

MICRO = 32
X, YH, CORE, ZH, ZL, YL = 4, 2, 2, 3, 4, 4
SIZES = (X, YH, CORE, ZH, ZL, YL)
NAMES = ("x", "yh", "core", "zh", "zl", "yl")
TOK, DIN, HD = 128, 4096, 512
SHARD = DIN // (X * YH * CORE)
PEERS = X * CORE
HALF = DIN // CORE
SOME = TOK // CORE
PIECES = YH * ZL * YL
ROWS = SHARD // (ZL * YL)
LANES = 128
FLAT = ROWS * HD // LANES
TALL = FLAT + 8
SCALE = float(TOK * X * YH * CORE * ZH * ZL * YL) ** -0.5
TOP = 13.0
SWAP = [(0, 1), (1, 0)]

VMEM = pl.BlockSpec(memory_space=pltpu.VMEM)
SMEM = pl.BlockSpec(memory_space=pltpu.SMEM)
ANY = pl.BlockSpec(memory_space=pl.ANY)
TINY, SMALL, LARGE = 8 * 1024 * 1024, 16 * 1024 * 1024, 60 * 1024 * 1024
bf16, f16, f32 = jnp.bfloat16, jnp.float16, jnp.float32


def pack_kernel(x_ref, core_ref, counts, acts, cot, packed, masked, lend, raw, kept, full, built, loan, sems):
    wide = DIN // X
    away = 1 - core_ref[0]
    first = pltpu.make_async_copy(cot, raw, sems.at[0])
    first.start()
    loads = [
        pltpu.make_async_copy(
            acts.at[:, x * wide:(x + 1) * wide], full.at[:, x * wide:(x + 1) * wide], sems.at[1 + x])
        for x in range(X)
    ]
    for load in loads:
        load.start()
    first.wait()
    rows = lax.broadcasted_iota(jnp.int32, (TOK, HD), 0)
    kept[...] = jnp.where(rows < counts[0] * MICRO, raw[...].astype(f32), 0.0).astype(bf16)
    stores = [pltpu.make_async_copy(kept, masked, sems.at[1 + X])]
    stores[0].start()
    for x in range(X):
        loads[x].wait()
        for side in range(CORE):
            peer = x * CORE + side
            for yh in range(YH):
                b = (x * YH + yh) * CORE + side
                built[peer, 0:TOK, yh * SHARD:(yh + 1) * SHARD] = full[:, b * SHARD:(b + 1) * SHARD]
            built[peer, TOK:TOK + SOME, :] = kept[side * SOME:(side + 1) * SOME, :]
        for yh in range(YH):
            start = pl.multiple_of(((x * YH + yh) * CORE + away) * SHARD, SHARD)
            loan[:, (x * YH + yh) * SHARD:(x * YH + yh + 1) * SHARD] = full[:, pl.ds(start, SHARD)]
        pieces = slice(x * CORE, (x + 1) * CORE)
        stores.append(pltpu.make_async_copy(built.at[pieces], packed.at[pieces], sems.at[2 + X + x]))
        stores[-1].start()
    loan[:, HALF:HALF + HD] = kept[...]
    stores.append(pltpu.make_async_copy(loan, lend, sems.at[2 + 2 * X]))
    stores[-1].start()
    for store in stores:
        store.wait()


def exponent(values):
    top = jnp.max(jnp.max(jnp.abs(values), axis=1, keepdims=True), axis=0, keepdims=True)
    return TOP - jnp.floor(jnp.log2(jnp.maximum(top, 2.0 ** -100)))


def encode(out, i, rows, power):
    for j in range(HD // LANES):
        out[i, j * ROWS:(j + 1) * ROWS, :] = rows[:, j * LANES:(j + 1) * LANES]
    out[i, FLAT:TALL, :] = jnp.broadcast_to(power, (TALL - FLAT, LANES))


def decode(ref, i):
    return ref[i, 0:FLAT, :] * jnp.exp2(-ref[i, FLAT:FLAT + 1, :])


def grad_kernel(core_ref, got, rest, pair, loan, out, same, same_loan, right, acc):
    core = core_ref[0]
    for i in range(PEERS):
        near = pl.multiple_of(i * TOK + core * SOME, SOME)
        far = pl.multiple_of(i * TOK + (1 - core) * SOME, SOME)
        right[pl.ds(near, SOME), :] = got[i, TOK:TOK + SOME, :]
        right[pl.ds(far, SOME), :] = rest[i]
    cols = 128
    for i in range(YH * SHARD // cols):
        left = got[:, 0:TOK, i * cols:(i + 1) * cols].reshape(PEERS * TOK, cols)
        acc[i * cols:(i + 1) * cols, :] = lax.dot_general(
            left, right[...], (((0,), (0,)), ((), ())), preferred_element_type=f32)
    power = exponent(acc[...])
    factor = jnp.exp2(power)
    for i in range(PIECES):
        encode(out, i, acc[i * ROWS:(i + 1) * ROWS, :] * factor, power)


def sum_kernel(parts, out):
    total = decode(parts, 0)
    for i in range(1, PIECES):
        total += decode(parts, i)
    for i in range(ZH):
        out[i] = total


def final_kernel(parts, out):
    total = parts[0]
    for i in range(1, ZH):
        total += parts[i]
    total = total * SCALE
    power = exponent(total)
    total = total * jnp.exp2(power)
    for i in range(ZL * YL):
        out[i, 0:FLAT, :] = total
        out[i, FLAT:TALL, :] = jnp.broadcast_to(power, (TALL - FLAT, LANES))


def unpack_kernel(got, out):
    for i in range(ZL * YL):
        value = decode(got, i)
        for j in range(HD // LANES):
            out[i * ROWS:(i + 1) * ROWS, j * LANES:(j + 1) * LANES] = value[j * ROWS:(j + 1) * ROWS, :]


def project_kernel(x_ref, core_ref, acts, masked, loan, after, w0, w1, w2, w3, part, grad, grad_away):
    x, core = x_ref[0], core_ref[0]
    kept = jnp.concatenate([masked[...], loan[:, HALF:HALF + HD]], axis=0)
    total = jnp.zeros((2 * TOK, HD), f32)
    for k, shards in enumerate((w0, w1, w2, w3)):
        group = lax.rem(x - k + X, X) * YH
        for yh in range(YH):
            w = shards[yh]
            near = pl.multiple_of(((group + yh) * CORE + core) * SHARD, SHARD)
            far = pl.multiple_of((group + yh) * SHARD, SHARD)
            rows = jnp.concatenate([acts[:, pl.ds(near, SHARD)], loan[:, pl.ds(far, SHARD)]], axis=0)
            total += jnp.dot(rows, w, preferred_element_type=f32)
            back = lax.dot_general(kept, w, (((1,), (1,)), ((), ())), preferred_element_type=f32).astype(bf16)
            cols = slice((k * YH + yh) * SHARD, (k * YH + yh + 1) * SHARD)
            grad[:, cols] = back[0:TOK]
            grad_away[:, cols] = back[TOK:2 * TOK]
    part[...] = total[0:TOK]
    top = total[TOK:2 * TOK].astype(bf16)
    grad_away[:, HALF:HALF + HD] = top
    grad_away[:, HALF + HD:HALF + 2 * HD] = (total[TOK:2 * TOK] - top.astype(f32)).astype(bf16)


def join_kernel(x_ref, core_ref, counts, part, grad, grad_away, projected, act_grad):
    x, core = x_ref[0], core_ref[0]
    rows = lax.broadcasted_iota(jnp.int32, (TOK, HD), 0)
    top = grad_away[:, HALF:HALF + HD].astype(f32)
    rest = grad_away[:, HALF + HD:HALF + 2 * HD].astype(f32)
    total = part[...] + (top + rest)
    projected[...] = jnp.where(rows < counts[0] * MICRO, total, 0.0).astype(bf16)
    for k in range(X):
        group = lax.rem(x - k + X, X) * YH
        for yh in range(YH):
            cols = slice((k * YH + yh) * SHARD, (k * YH + yh + 1) * SHARD)
            near = pl.multiple_of(((group + yh) * CORE + core) * SHARD, SHARD)
            far = pl.multiple_of(((group + yh) * CORE + 1 - core) * SHARD, SHARD)
            act_grad[:, pl.ds(near, SHARD)] = grad[:, cols]
            act_grad[:, pl.ds(far, SHARD)] = grad_away[:, cols]


def sds(shape, dtype):
    return jax.ShapeDtypeStruct(shape, dtype)


def call(body, outs, ins, out_specs, scratch=(), name=None, limit=SMALL, **more):
    return pl.pallas_call(
        body, out_shape=outs, in_specs=ins, out_specs=out_specs, scratch_shapes=list(scratch),
        compiler_params=pltpu.CompilerParams(vmem_limit_bytes=limit), name=name, **more)


def exchange(value, axes):
    return lax.all_to_all(value, axes, 0, 0, tiled=True)


def per_device(acts, cotangent, kv_weight, batch_counts):
    x, core = lax.axis_index("x"), lax.axis_index("core")
    yh, yl = lax.axis_index("yh"), lax.axis_index("yl")
    dma = pltpu.SemaphoreType.DMA

    packed, masked, lend = call(
        pack_kernel,
        (sds((PEERS, TOK + SOME, HD), bf16), sds((TOK, HD), bf16), sds((TOK, HALF + HD), bf16)),
        [SMEM, SMEM, SMEM, ANY, ANY], (ANY, ANY, ANY),
        (pltpu.VMEM((TOK, HD), bf16), pltpu.VMEM((TOK, HD), bf16), pltpu.VMEM((TOK, DIN), bf16),
         pltpu.VMEM((PEERS, TOK + SOME, HD), bf16), pltpu.VMEM((TOK, HALF + HD), bf16), dma((3 + 2 * X,))),
        "pack", LARGE,
    )(x.reshape(1), core.reshape(1), batch_counts, acts, cotangent)
    got = exchange(packed, ("x", "core"))
    rest = lax.ppermute(got[:, TOK:TOK + SOME, :], "core", SWAP)

    near = lax.ppermute(kv_weight, ("yh", "yl"), [(4, 3), (7, 0), (3, 4), (0, 7)])
    far = lax.ppermute(kv_weight, ("yh", "yl"), [(4, 2), (7, 1), (3, 5), (0, 6)])
    twin = jnp.where((yl == 0) | (yl == YL - 1), near, far)
    pair = jnp.where(yh == 0, jnp.stack([kv_weight, twin]), jnp.stack([twin, kv_weight]))
    loan = lax.ppermute(lend, "core", SWAP)

    partial, pair, loan = call(
        grad_kernel,
        (sds((PIECES, TALL, LANES), f32), sds((YH, SHARD, HD), bf16), sds((TOK, HALF + HD), bf16)),
        [SMEM, VMEM, VMEM, ANY, ANY], (VMEM, ANY, ANY),
        (pltpu.VMEM((PEERS * TOK, HD), bf16), pltpu.VMEM((YH * SHARD, HD), f32)), "grad",
        input_output_aliases={3: 1, 4: 2},
    )(core.reshape(1), got, rest, pair, loan)

    parts = exchange(partial.astype(f16), ("yh", "zl", "yl"))
    turned = [lax.ppermute(pair, "x", [(i, (i + k) % X) for i in range(X)]) for k in range(1, X)]
    piece = call(sum_kernel, sds((ZH, FLAT, LANES), f32), [VMEM], VMEM, name="sum", limit=TINY)(parts.astype(f32))
    pieces = exchange(piece, "zh")
    ready = call(
        final_kernel, sds((ZL * YL, TALL, LANES), f32), [VMEM], VMEM, name="final", limit=TINY)(pieces)
    whole = exchange(ready.astype(f16), ("zl", "yl"))

    part, grad, grad_away = call(
        project_kernel,
        (sds((TOK, HD), f32), sds((TOK, HALF), bf16), sds((TOK, HALF + 2 * HD), bf16)),
        [SMEM, SMEM, VMEM, VMEM, VMEM, ANY] + [VMEM] * 4, (VMEM,) * 3, (), "project", SMALL,
        cost_estimate=pl.CostEstimate(
            flops=4 * TOK * DIN * HD, bytes_accessed=2 * (2 * TOK * DIN + DIN * HD), transcendentals=0),
    )(x.reshape(1), core.reshape(1), acts, masked, loan, piece, pair, *turned)
    grad_away = lax.ppermute(grad_away, "core", SWAP)
    projected, act_grad = call(
        join_kernel, (sds((TOK, HD), bf16), sds((TOK, DIN), bf16)),
        [SMEM, SMEM, SMEM] + [VMEM] * 3, (VMEM, VMEM), (), "join", SMALL,
    )(x.reshape(1), core.reshape(1), batch_counts, part, grad, grad_away)

    weight_grad = call(
        unpack_kernel, sds((SHARD, HD), f32), [VMEM], VMEM, name="unpack", limit=TINY)(whole.astype(f32))
    return projected, act_grad, weight_grad


def solution(mesh):
    inner = Mesh(mesh.devices.reshape(SIZES), NAMES)
    return jax.shard_map(
        per_device,
        mesh=inner,
        in_specs=(P(NAMES, None), P(NAMES, None), P(("x", "yh", "core"), None), P(NAMES)),
        out_specs=(P(NAMES, None), P(NAMES, None), P(("x", "yh", "core"), None)),
        check_vma=False,
    )
```

```python
import jax
import jax.numpy as jnp
from jax import lax
from jax.experimental import pallas as pl
from jax.experimental.pallas import tpu as pltpu
from jax.sharding import Mesh, PartitionSpec as P

MICRO = 32
X, YH, CORE, ZH, ZL, YL = 4, 2, 2, 3, 4, 4
SIZES = (X, YH, CORE, ZH, ZL, YL)
NAMES = ("x", "yh", "core", "zh", "zl", "yl")
TOK, DIN, HD = 128, 4096, 512
SHARD = DIN // (X * YH * CORE)
PEERS = X * CORE
HALF = DIN // CORE
SOME = TOK // CORE
PIECES = YH * ZL * YL
ROWS = SHARD // (ZL * YL)
LANES = 128
FLAT = ROWS * HD // LANES
TALL = FLAT + 8
SCALE = float(TOK * X * YH * CORE * ZH * ZL * YL) ** -0.5
TOP = 13.0
SWAP = [(0, 1), (1, 0)]

VMEM = pl.BlockSpec(memory_space=pltpu.VMEM)
SMEM = pl.BlockSpec(memory_space=pltpu.SMEM)
ANY = pl.BlockSpec(memory_space=pl.ANY)
TINY, SMALL, LARGE = 8 * 1024 * 1024, 16 * 1024 * 1024, 60 * 1024 * 1024
bf16, f16, f32 = jnp.bfloat16, jnp.float16, jnp.float32


def pack_kernel(x_ref, core_ref, counts, acts, cot, packed, masked, lend, raw, kept, full, built, loan, sems):
    wide = DIN // X
    away = 1 - core_ref[0]
    first = pltpu.make_async_copy(cot, raw, sems.at[0])
    first.start()
    loads = [
        pltpu.make_async_copy(
            acts.at[:, x * wide:(x + 1) * wide], full.at[:, x * wide:(x + 1) * wide], sems.at[1 + x])
        for x in range(X)
    ]
    for load in loads:
        load.start()
    first.wait()
    rows = lax.broadcasted_iota(jnp.int32, (TOK, HD), 0)
    kept[...] = jnp.where(rows < counts[0] * MICRO, raw[...].astype(f32), 0.0).astype(bf16)
    stores = [pltpu.make_async_copy(kept, masked, sems.at[1 + X])]
    stores[0].start()
    for x in range(X):
        loads[x].wait()
        for side in range(CORE):
            peer = x * CORE + side
            for yh in range(YH):
                b = (x * YH + yh) * CORE + side
                built[peer, 0:TOK, yh * SHARD:(yh + 1) * SHARD] = full[:, b * SHARD:(b + 1) * SHARD]
            built[peer, TOK:TOK + SOME, :] = kept[side * SOME:(side + 1) * SOME, :]
        for yh in range(YH):
            start = pl.multiple_of(((x * YH + yh) * CORE + away) * SHARD, SHARD)
            loan[:, (x * YH + yh) * SHARD:(x * YH + yh + 1) * SHARD] = full[:, pl.ds(start, SHARD)]
        pieces = slice(x * CORE, (x + 1) * CORE)
        stores.append(pltpu.make_async_copy(built.at[pieces], packed.at[pieces], sems.at[2 + X + x]))
        stores[-1].start()
    loan[:, HALF:HALF + HD] = kept[...]
    stores.append(pltpu.make_async_copy(loan, lend, sems.at[2 + 2 * X]))
    stores[-1].start()
    for store in stores:
        store.wait()


def exponent(values):
    top = jnp.max(jnp.max(jnp.abs(values), axis=1, keepdims=True), axis=0, keepdims=True)
    return TOP - jnp.floor(jnp.log2(jnp.maximum(top, 2.0 ** -100)))


def encode(out, i, rows, power):
    for j in range(HD // LANES):
        out[i, j * ROWS:(j + 1) * ROWS, :] = rows[:, j * LANES:(j + 1) * LANES]
    out[i, FLAT:TALL, :] = jnp.broadcast_to(power, (TALL - FLAT, LANES))


def decode(ref, i):
    return ref[i, 0:FLAT, :] * jnp.exp2(-ref[i, FLAT:FLAT + 1, :])


def half_grad(got, rows, core, acc, first):
    cols = 128
    start = pl.multiple_of(core * SOME, SOME)
    right = rows.reshape(PEERS * SOME, HD)
    for i in range(YH * SHARD // cols):
        left = got[:, pl.ds(start, SOME), i * cols:(i + 1) * cols].reshape(PEERS * SOME, cols)
        part = lax.dot_general(left, right, (((0,), (0,)), ((), ())), preferred_element_type=f32)
        span = slice(i * cols, (i + 1) * cols)
        acc[span, :] = part + first[span, :] if first is not None else part


def near_kernel(core_ref, got, acc):
    half_grad(got, got[:, TOK:TOK + SOME, :], core_ref[0], acc, None)


def grad_kernel(core_ref, got, first, rest, pair, loan, out, same, same_loan, acc):
    half_grad(got, rest[...], 1 - core_ref[0], acc, first)
    power = exponent(acc[...])
    factor = jnp.exp2(power)
    for i in range(PIECES):
        encode(out, i, acc[i * ROWS:(i + 1) * ROWS, :] * factor, power)


def sum_kernel(parts, out):
    total = decode(parts, 0)
    for i in range(1, PIECES):
        total += decode(parts, i)
    for i in range(ZH):
        out[i] = total


def final_kernel(parts, out):
    total = parts[0]
    for i in range(1, ZH):
        total += parts[i]
    total = total * SCALE
    power = exponent(total)
    total = total * jnp.exp2(power)
    for i in range(ZL * YL):
        out[i, 0:FLAT, :] = total
        out[i, FLAT:TALL, :] = jnp.broadcast_to(power, (TALL - FLAT, LANES))


def unpack_kernel(got, out):
    for i in range(ZL * YL):
        value = decode(got, i)
        for j in range(HD // LANES):
            out[i * ROWS:(i + 1) * ROWS, j * LANES:(j + 1) * LANES] = value[j * ROWS:(j + 1) * ROWS, :]


def project_kernel(x_ref, core_ref, acts, masked, loan, after, w0, w1, w2, w3, part, grad, grad_away):
    x, core = x_ref[0], core_ref[0]
    kept = jnp.concatenate([masked[...], loan[:, HALF:HALF + HD]], axis=0)
    total = jnp.zeros((2 * TOK, HD), f32)
    for k, shards in enumerate((w0, w1, w2, w3)):
        group = lax.rem(x - k + X, X) * YH
        for yh in range(YH):
            w = shards[yh]
            near = pl.multiple_of(((group + yh) * CORE + core) * SHARD, SHARD)
            far = pl.multiple_of((group + yh) * SHARD, SHARD)
            rows = jnp.concatenate([acts[:, pl.ds(near, SHARD)], loan[:, pl.ds(far, SHARD)]], axis=0)
            total += jnp.dot(rows, w, preferred_element_type=f32)
            back = lax.dot_general(kept, w, (((1,), (1,)), ((), ())), preferred_element_type=f32).astype(bf16)
            cols = slice((k * YH + yh) * SHARD, (k * YH + yh + 1) * SHARD)
            grad[:, cols] = back[0:TOK]
            grad_away[:, cols] = back[TOK:2 * TOK]
    part[...] = total[0:TOK]
    top = total[TOK:2 * TOK].astype(bf16)
    grad_away[:, HALF:HALF + HD] = top
    grad_away[:, HALF + HD:HALF + 2 * HD] = (total[TOK:2 * TOK] - top.astype(f32)).astype(bf16)


def join_kernel(x_ref, core_ref, counts, part, grad, grad_away, projected, act_grad):
    x, core = x_ref[0], core_ref[0]
    rows = lax.broadcasted_iota(jnp.int32, (TOK, HD), 0)
    top = grad_away[:, HALF:HALF + HD].astype(f32)
    rest = grad_away[:, HALF + HD:HALF + 2 * HD].astype(f32)
    total = part[...] + (top + rest)
    projected[...] = jnp.where(rows < counts[0] * MICRO, total, 0.0).astype(bf16)
    for k in range(X):
        group = lax.rem(x - k + X, X) * YH
        for yh in range(YH):
            cols = slice((k * YH + yh) * SHARD, (k * YH + yh + 1) * SHARD)
            near = pl.multiple_of(((group + yh) * CORE + core) * SHARD, SHARD)
            far = pl.multiple_of(((group + yh) * CORE + 1 - core) * SHARD, SHARD)
            act_grad[:, pl.ds(near, SHARD)] = grad[:, cols]
            act_grad[:, pl.ds(far, SHARD)] = grad_away[:, cols]


def sds(shape, dtype):
    return jax.ShapeDtypeStruct(shape, dtype)


def call(body, outs, ins, out_specs, scratch=(), name=None, limit=SMALL, **more):
    return pl.pallas_call(
        body, out_shape=outs, in_specs=ins, out_specs=out_specs, scratch_shapes=list(scratch),
        compiler_params=pltpu.CompilerParams(vmem_limit_bytes=limit), name=name, **more)


def exchange(value, axes):
    return lax.all_to_all(value, axes, 0, 0, tiled=True)


def per_device(acts, cotangent, kv_weight, batch_counts):
    x, core = lax.axis_index("x"), lax.axis_index("core")
    yh, yl = lax.axis_index("yh"), lax.axis_index("yl")
    dma = pltpu.SemaphoreType.DMA

    packed, masked, lend = call(
        pack_kernel,
        (sds((PEERS, TOK + SOME, HD), bf16), sds((TOK, HD), bf16), sds((TOK, HALF + HD), bf16)),
        [SMEM, SMEM, SMEM, ANY, ANY], (ANY, ANY, ANY),
        (pltpu.VMEM((TOK, HD), bf16), pltpu.VMEM((TOK, HD), bf16), pltpu.VMEM((TOK, DIN), bf16),
         pltpu.VMEM((PEERS, TOK + SOME, HD), bf16), pltpu.VMEM((TOK, HALF + HD), bf16), dma((3 + 2 * X,))),
        "pack", LARGE,
    )(x.reshape(1), core.reshape(1), batch_counts, acts, cotangent)
    got = exchange(packed, ("x", "core"))
    rest = lax.ppermute(got[:, TOK:TOK + SOME, :], "core", SWAP)

    near = lax.ppermute(kv_weight, ("yh", "yl"), [(4, 3), (7, 0), (3, 4), (0, 7)])
    far = lax.ppermute(kv_weight, ("yh", "yl"), [(4, 2), (7, 1), (3, 5), (0, 6)])
    twin = jnp.where((yl == 0) | (yl == YL - 1), near, far)
    pair = jnp.where(yh == 0, jnp.stack([kv_weight, twin]), jnp.stack([twin, kv_weight]))
    loan = lax.ppermute(lend, "core", SWAP)

    first = call(near_kernel, sds((YH * SHARD, HD), f32), [SMEM, VMEM], VMEM, name="near")(core.reshape(1), got)
    partial, pair, loan = call(
        grad_kernel,
        (sds((PIECES, TALL, LANES), f32), sds((YH, SHARD, HD), bf16), sds((TOK, HALF + HD), bf16)),
        [SMEM, VMEM, VMEM, VMEM, ANY, ANY], (VMEM, ANY, ANY),
        (pltpu.VMEM((YH * SHARD, HD), f32),), "grad",
        input_output_aliases={4: 1, 5: 2},
    )(core.reshape(1), got, first, rest, pair, loan)

    parts = exchange(partial.astype(f16), ("yh", "zl", "yl"))
    turned = [lax.ppermute(pair, "x", [(i, (i + k) % X) for i in range(X)]) for k in range(1, X)]
    piece = call(sum_kernel, sds((ZH, FLAT, LANES), f32), [VMEM], VMEM, name="sum", limit=TINY)(parts.astype(f32))
    pieces = exchange(piece, "zh")
    ready = call(
        final_kernel, sds((ZL * YL, TALL, LANES), f32), [VMEM], VMEM, name="final", limit=TINY)(pieces)
    whole = exchange(ready.astype(f16), ("zl", "yl"))

    part, grad, grad_away = call(
        project_kernel,
        (sds((TOK, HD), f32), sds((TOK, HALF), bf16), sds((TOK, HALF + 2 * HD), bf16)),
        [SMEM, SMEM, VMEM, VMEM, VMEM, ANY] + [VMEM] * 4, (VMEM,) * 3, (), "project", SMALL,
        cost_estimate=pl.CostEstimate(
            flops=4 * TOK * DIN * HD, bytes_accessed=2 * (2 * TOK * DIN + DIN * HD), transcendentals=0),
    )(x.reshape(1), core.reshape(1), acts, masked, loan, piece, pair, *turned)
    grad_away = lax.ppermute(grad_away, "core", SWAP)
    projected, act_grad = call(
        join_kernel, (sds((TOK, HD), bf16), sds((TOK, DIN), bf16)),
        [SMEM, SMEM, SMEM] + [VMEM] * 3, (VMEM, VMEM), (), "join", SMALL,
    )(x.reshape(1), core.reshape(1), batch_counts, part, grad, grad_away)

    weight_grad = call(
        unpack_kernel, sds((SHARD, HD), f32), [VMEM], VMEM, name="unpack", limit=TINY)(whole.astype(f32))
    return projected, act_grad, weight_grad


def solution(mesh):
    inner = Mesh(mesh.devices.reshape(SIZES), NAMES)
    return jax.shard_map(
        per_device,
        mesh=inner,
        in_specs=(P(NAMES, None), P(NAMES, None), P(("x", "yh", "core"), None), P(NAMES)),
        out_specs=(P(NAMES, None), P(NAMES, None), P(("x", "yh", "core"), None)),
        check_vma=False,
    )
```
